768 devices in a mesh: row: 8 (over z_hi, core), col: 96 (over x, y, z_lo).
Axes of the slice: x: 4, y: 8, z: 12 (z_hi: 4, z_lo: 3; z = z_hi * 3 + z_lo), core: 2. Of those that a mesh axis runs over, the one named last changes fastest.
Arguments:
- left_blocks: bfloat16 [64, 192, 128, 128], P('row', 'col'), may hold values from -6 to 6
- left_columns: int32 [64, 192], P('row', 'col'), may hold values from 0 to 3, as said below
- left_count: int32 [64, 96], P('row', 'col'), may hold values from 1 to 2, as said below
- right_blocks: bfloat16 [32, 192, 128, 128], P('row', 'col'), may hold values from -0.375 to 0.375
- right_columns: int32 [32, 192], P('row', 'col'), may hold values from 0 to 7, as said below
- right_count: int32 [32, 96], P('row', 'col'), may hold values from 1 to 2, as said below
- out_columns: int32 [64, 384], P('row', 'col'), may hold values from 0 to 7, as said below
- out_count: int32 [64, 96], P('row', 'col'), may hold values from 1 to 4, as said below
- atom_owner: int32 [12, 32], replicated, may hold values from 0 to 7, as said below
Outputs:
- product: bfloat16 [64, 384, 128, 128], P('row', 'col')
The draws below stay inside these ranges and needn't reach their ends.
Inputs may be any that keep to these rules, and one draw needn't show every extreme that they name: `left_columns`: within one row and one grid column the 2 entries are distinct. `left_count`: rows 0, 8, 16 and so on have the full count in every grid column. `right_columns`: within one row and one grid column the 2 entries are distinct. `right_count`: rows 0, 4, 8 and so on have the full count in every grid column. `out_columns`: within one row and one grid column the 4 entries are distinct. `out_count`: rows 0, 8, 16 and so on have the full count in every grid column. `atom_owner`: in each region every owner holds exactly 4 block rows, and the 4 rows of one panel (rows p * 4 to p * 4 + 3) have distinct owners.
All inputs are finite; a program needn't handle non-finite values.
Results may differ from the reference program's by a relative error of at most 0.001.
Values may be sent and summed in bfloat16 or wider, within the bound.
A program may use at most 64 MiB of HBM per device.

```python
import jax
import jax.numpy as jnp
from jax import lax

BLOCK = 128
ROW_BLOCKS = 8
PANEL = 4
LEFT_SLOTS = 2
RIGHT_SLOTS = 2
OUT_WIDTH = 8
OUT_SLOTS = 4
GRID = 8
REGIONS = 12
WIN_ROWS = 64
CONTRACT = 32
N_COL = 96


def distinct_pick(key, shape, choose, total):
    scores = jax.random.randint(key, shape + (total,), 0, 1 << 20) * total + lax.broadcasted_iota(jnp.int32, shape + (total,), len(shape))
    order = jnp.argsort(scores, axis=-1, stable=True)
    return order[..., :choose].astype(jnp.int32)


def counts_with_full(key, rows, period, most):
    counts = jax.random.randint(key, (rows, N_COL), 1, most + 1)
    first = lax.broadcasted_iota(jnp.int32, (rows, N_COL), 0) % period == 0
    return jnp.where(first, most, counts).astype(jnp.int32)


def draw_left_columns(key, part):
    key = jax.random.fold_in(key, 1)
    return distinct_pick(key, (WIN_ROWS, N_COL), LEFT_SLOTS, PANEL).reshape(WIN_ROWS, N_COL * LEFT_SLOTS)


def draw_left_count(key, part):
    key = jax.random.fold_in(key, 2)
    return counts_with_full(key, WIN_ROWS, ROW_BLOCKS, LEFT_SLOTS)


def draw_right_columns(key, part):
    key = jax.random.fold_in(key, 3)
    return distinct_pick(key, (CONTRACT, N_COL), RIGHT_SLOTS, OUT_WIDTH).reshape(CONTRACT, N_COL * RIGHT_SLOTS)


def draw_right_count(key, part):
    key = jax.random.fold_in(key, 4)
    return counts_with_full(key, CONTRACT, PANEL, RIGHT_SLOTS)


def draw_out_columns(key, part):
    key = jax.random.fold_in(key, 5)
    return distinct_pick(key, (WIN_ROWS, N_COL), OUT_SLOTS, OUT_WIDTH).reshape(WIN_ROWS, N_COL * OUT_SLOTS)


def draw_out_count(key, part):
    key = jax.random.fold_in(key, 6)
    return counts_with_full(key, WIN_ROWS, ROW_BLOCKS, OUT_SLOTS)


def draw_atom_owner(key, part):
    key = jax.random.fold_in(key, 7)
    first, second = jax.random.split(key)
    shuffle = distinct_pick(first, (REGIONS,), GRID, GRID)
    within = distinct_pick(second, (REGIONS, GRID), PANEL, PANEL)
    picked = jnp.take_along_axis(shuffle[:, None, :], within, axis=2)
    panels = lax.broadcasted_iota(jnp.int32, (REGIONS, GRID, PANEL), 1)
    return ((panels + picked) % GRID).reshape(REGIONS, CONTRACT).astype(jnp.int32)


def levels(own_key, dims, cuts, low, high):
    level = 1.0
    for dim, blocks in cuts:
        steps = jax.random.uniform(jax.random.fold_in(jax.random.fold_in(own_key, 6), dim), (blocks,), jnp.float32, low / len(cuts), high / len(cuts))
        level = level * jnp.repeat(jnp.exp(steps), dims[dim] // blocks).reshape((-1,) + (1,) * (len(dims) - 1 - dim))
    return level


def noise(own_key, extent, spread, reach, shards=(), held_as=jnp.bfloat16):
    values = spread * jax.random.normal(own_key, extent, jnp.float32)
    if shards:
        values = values * levels(own_key, extent, shards, -0.22, 0.18)
    return jnp.clip(values, -reach, reach).astype(held_as)


def setup_inputs(seed: int = 0) -> dict:
    splits = jax.random.split(jax.random.key(seed), 10)
    return {
        "left_blocks": noise(splits[0], (WIN_ROWS, N_COL * LEFT_SLOTS, BLOCK, BLOCK), 1.0, 6.0, ((0, 8), (1, 96))),
        "left_columns": draw_left_columns(jax.random.fold_in(splits[9], 71), 0),
        "left_count": draw_left_count(jax.random.fold_in(splits[9], 71), 0),
        "right_blocks": noise(splits[3], (CONTRACT, N_COL * RIGHT_SLOTS, BLOCK, BLOCK), (2 * BLOCK) ** -0.5, 0.375, ((0, 8), (1, 96))),
        "right_columns": draw_right_columns(jax.random.fold_in(splits[9], 71), 0),
        "right_count": draw_right_count(jax.random.fold_in(splits[9], 71), 0),
        "out_columns": draw_out_columns(jax.random.fold_in(splits[9], 71), 0),
        "out_count": draw_out_count(jax.random.fold_in(splits[9], 71), 0),
        "atom_owner": draw_atom_owner(jax.random.fold_in(splits[9], 71), 0),
    }


def panel_product(left_state, right_state, out_columns):
    left_blocks, left_columns, left_count = left_state
    right_blocks, right_columns, right_count = right_state
    rows, slots = left_columns.shape
    panel, width = right_columns.shape
    block = right_blocks.shape[-1]
    left_live = lax.broadcasted_iota(jnp.int32, (rows, slots), 1) < left_count
    right_live = lax.broadcasted_iota(jnp.int32, (panel, width), 1) < right_count
    row_columns = right_columns[left_columns]
    row_live = right_live[left_columns]
    match = (row_columns[:, :, None, :] == out_columns[:, None, :, None]) & row_live[:, :, None, :]
    position = jnp.sum(jnp.where(match, lax.broadcasted_iota(jnp.int32, match.shape, 3), 0), axis=3).astype(jnp.int32)
    found = jnp.any(match, axis=3) & left_live[:, :, None]
    flat = (left_columns[:, :, None] * width + position).astype(jnp.int32)
    picked = right_blocks.reshape(panel * width, block, block)[flat]
    picked = jnp.where(found[:, :, :, None, None], picked, jnp.zeros((), right_blocks.dtype))
    return jnp.einsum("iaxy,iacyz->icxz", left_blocks.astype(jnp.float32), picked.astype(jnp.float32),
                      precision=lax.Precision.HIGHEST)


def reference(left_blocks, left_columns, left_count, right_blocks, right_columns, right_count, out_columns, out_count, atom_owner):
    order = jnp.arange(CONTRACT, dtype=jnp.int32)
    earlier = (atom_owner[:, :, None] == atom_owner[:, None, :]) & (order[None, None, :] < order[None, :, None])
    rank = jnp.sum(earlier.astype(jnp.int32), axis=2).astype(jnp.int32)
    source = (atom_owner * PANEL + rank).astype(jnp.int32)
    dev_rows = jnp.arange(GRID, dtype=jnp.int32)
    columns = jnp.arange(N_COL, dtype=jnp.int32)
    cannon = columns // REGIONS
    region = columns % REGIONS
    k_index = (((dev_rows[:, None] + cannon[None, :]) % GRID) * PANEL)[:, None, :] + jnp.arange(PANEL, dtype=jnp.int32)[None, :, None]
    src = source[region[None, None, :], k_index].astype(jnp.int32)
    column_index = jnp.broadcast_to(columns[None, None, :], src.shape)
    right_all = right_blocks.reshape(CONTRACT, N_COL, RIGHT_SLOTS, BLOCK, BLOCK)[src, column_index]
    right_cols = right_columns.reshape(CONTRACT, N_COL, RIGHT_SLOTS)[src, column_index]
    right_cnt = right_count[src, column_index]
    left_all = left_blocks.reshape(GRID, ROW_BLOCKS, N_COL, LEFT_SLOTS, BLOCK, BLOCK)
    left_cols = left_columns.reshape(GRID, ROW_BLOCKS, N_COL, LEFT_SLOTS)
    left_cnt = left_count.reshape(GRID, ROW_BLOCKS, N_COL)
    out_cols = out_columns.reshape(GRID, ROW_BLOCKS, N_COL, OUT_SLOTS)
    out_cnt = out_count.reshape(GRID, ROW_BLOCKS, N_COL)

    def device(entry):
        grid_row = entry // N_COL
        grid_col = entry % N_COL
        cannon_col = grid_col // REGIONS
        reg = grid_col % REGIONS
        wanted = out_cols[grid_row, :, grid_col]
        total = jnp.zeros((ROW_BLOCKS, OUT_SLOTS, BLOCK, BLOCK), jnp.float32)
        for panel_id in range(GRID):
            left_col = ((panel_id - grid_row) % GRID) * REGIONS + reg
            left_state = (left_all[grid_row, :, left_col], left_cols[grid_row, :, left_col], left_cnt[grid_row, :, left_col][:, None])
            right_row = (panel_id - cannon_col) % GRID
            right_state = (right_all[right_row, :, grid_col], right_cols[right_row, :, grid_col], right_cnt[right_row, :, grid_col][:, None])
            total = total + panel_product(left_state, right_state, wanted)
        live = lax.broadcasted_iota(jnp.int32, (ROW_BLOCKS, OUT_SLOTS), 1) < out_cnt[grid_row, :, grid_col][:, None]
        return jnp.where(live[:, :, None, None], total, jnp.zeros((), jnp.float32)).astype(jnp.bfloat16)

    blocks = lax.map(device, jnp.arange(GRID * N_COL, dtype=jnp.int32))
    blocks = blocks.reshape(GRID, N_COL, ROW_BLOCKS, OUT_SLOTS, BLOCK, BLOCK).transpose(0, 2, 1, 3, 4, 5)
    return blocks.reshape(WIN_ROWS, N_COL * OUT_SLOTS, BLOCK, BLOCK)
```

```python
import functools

import jax
import jax.numpy as jnp
from jax import lax
from jax.experimental import pallas as pl
from jax.experimental.pallas import tpu as pltpu
from jax.sharding import PartitionSpec as P

MESH = pl.DeviceIdType.MESH
ROWS, SLOTS, OUT, PANEL, BLOCK = 8, 2, 4, 4, 128
HALF = ROWS // 2
STEP = 2
N_COPIES = 160
ZERO = 64
PARTS = ("x", "y", "z", "meta", "compute")


def kernel(
    parts,
    left_hbm, lcol, lcount, right_hbm, rcol, rcount, ocol, ocount, owner,
    out_hbm,
    left, relay, right, acc, stage,
    lcode, rcode, ocode, place, pick,
    send_sem, recv_sem, local_sem, out_sem,
):
    r = lax.axis_index("row")
    c = lax.axis_index("col")
    z, core = r // 2, r % 2
    x, y, low = c // 24, (c // 3) % 8, c % 3

    def at_q(dx, dy):
        return (r, ((x + dx) % 4) * 24 + ((y + dy) % 8) * 3 + low)

    def at_row(dz, dcore):
        return (((z + dz) % 4) * 2 + (core + dcore) % 2, c)

    q_peers = [(dy * 4 + dx, at_q(dx, 4 * dy)) for dy in range(2) for dx in range(4)][1:]
    row_peers = [(dz * 2 + dc, at_row(dz, dc)) for dz in range(4) for dc in range(2)][1:]
    east, west = at_q(1, 0), at_q(3, 0)
    north, south = at_q(0, 2), at_q(0, 6)
    up, down, twin = at_row(1, 0), at_row(3, 0), at_row(0, 1)

    barrier = pltpu.get_barrier_semaphore()
    greeted = [d for _, d in q_peers] + [d for _, d in row_peers] + [north, south]
    for device in greeted:
        pl.semaphore_signal(barrier, inc=1, device_id=device, device_id_type=MESH)
    own_left = pltpu.make_async_copy(left_hbm, left.at[0], local_sem.at[0])
    own_left.start()
    own_right = pltpu.make_async_copy(right_hbm, right.at[pl.ds(0, 8)], local_sem.at[1])
    own_right.start()
    for i in range(ROWS):
        for s in range(SLOTS):
            lcode[0, i * 2 + s] = jnp.where(s < lcount[i, 0], lcol[i, s], -1)
        for t in range(OUT):
            ocode[i * 4 + t] = jnp.where(t < ocount[i, 0], ocol[i, t], -1)
    for k in range(PANEL):
        for s in range(2):
            rcode[0, k * 2 + s] = jnp.where(s < rcount[k, 0], rcol[k, s], -2)
    pl.semaphore_wait(barrier, len(greeted))

    sent = []

    def remote(src, dst, device):
        n = len(sent)
        copy = pltpu.make_async_remote_copy(
            src_ref=src, dst_ref=dst, send_sem=send_sem.at[n], recv_sem=recv_sem.at[n],
            device_id=device, device_id_type=MESH,
        )
        copy.start()
        sent.append(copy)
        return copy

    def rows(first):
        return pl.ds(first, STEP)

    alpha = list(range(0, HALF, STEP))
    beta = list(range(HALF, ROWS, STEP))
    n = len(alpha)
    events = []
    waits = {d: [] for d in range(8)}
    right_waits = []

    def ring(d, first, east_copy, west_copy, when):
        if first in alpha:
            def forward():
                east_copy.wait_recv()
                waits[d + 2].append((first, remote(left.at[d + 3, rows(first)], left.at[d + 2, rows(first)], east)))
            events.append((when, forward))
            waits[d + 1].append((first, west_copy))
        else:
            def forward():
                west_copy.wait_recv()
                waits[d + 2].append((first, remote(left.at[d + 1, rows(first)], left.at[d + 2, rows(first)], west)))
            events.append((when, forward))
            waits[d + 3].append((first, east_copy))

    if "y" in parts:
        relayed = []
        for j in range(n):
            relayed.append((
                remote(left_hbm.at[rows(alpha[j])], relay.at[rows(alpha[j])], north),
                remote(left_hbm.at[rows(beta[j])], relay.at[rows(beta[j])], south)))
    if "x" in parts:
        ecopies, wcopies = {}, {}
        for a, b in zip(alpha + beta, beta + alpha):
            ecopies[a] = remote(left_hbm.at[rows(a)], left.at[3, rows(a)], east)
            wcopies[b] = remote(left_hbm.at[rows(b)], left.at[1, rows(b)], west)
        for j in range(n):
            ring(0, alpha[j], ecopies[alpha[j]], wcopies[alpha[j]], 5.2 * (j + 1) / n)
            ring(0, beta[j], ecopies[beta[j]], wcopies[beta[j]], 5.2 * (j + 1) / n)
    if "z" in parts:
        zparts = [(0, 4), (4, 4)]
        ucopies, dcopies = {}, {}
        for a, b in zip(zparts, zparts[::-1]):
            ucopies[a] = remote(right_hbm.at[pl.ds(*a)], right.at[pl.ds(48 + a[0], a[1])], up)
            dcopies[b] = remote(right_hbm.at[pl.ds(*b)], right.at[pl.ds(16 + b[0], b[1])], down)
        right_waits.append(remote(right_hbm, right.at[pl.ds(8, 8)], twin))

        def share(copy, at, size):
            copy.wait_recv()
            right_waits.append(remote(right.at[pl.ds(at, size)], right.at[pl.ds(at + 8, size)], twin))

        def zring(copy, at, size, to, when, on):
            def forward():
                copy.wait_recv()
                if on is not None:
                    passed = remote(right.at[pl.ds(at, size)], right.at[pl.ds(to, size)], on)
                    events2.append((passed, to, size))
                right_waits.append(remote(right.at[pl.ds(at, size)], right.at[pl.ds(at + 8, size)], twin))
            events.append((when, forward))

        events2 = []
        a, b = zparts
        zring(ucopies[a], 48 + a[0], a[1], 32 + a[0], 8.0, up)
        zring(dcopies[b], 16 + b[0], b[1], 32 + b[0], 8.0, down)
        zring(ucopies[b], 48 + b[0], b[1], None, 16.0, None)
        zring(dcopies[a], 16 + a[0], a[1], None, 16.0, None)

        def last():
            for passed, to, size in events2:
                share(passed, to, size)
        events.append((24.0, last))
    if "meta" in parts:
        metas = [remote(lcode.at[0], lcode.at[slot_of(d)], device) for d, device in q_peers]
        metas += [remote(rcode.at[0], rcode.at[slot_of_row(d)], device) for d, device in row_peers]

        def indices():
            region = (y % 4) * 3 + low

            @pl.loop(0, 32)
            def _(k):
                o = owner[region, k]
                rank = jnp.int32(0)
                for e in range(32):
                    rank += jnp.where((owner[region, e] == o) & (e < k), 1, 0)
                oz, oc = o // 2, o % 2
                place[k] = (((oz - z + 4) % 4) * 2 + (oc + core) % 2) * 4 + jnp.minimum(rank, 3)

            for copy in metas:
                copy.wait_recv()

            @pl.loop(0, 64)
            def _(n):
                d, i = n // 8, n % 8
                q = ((x + d % 4) % 4) * 2 + (y // 4 + d // 4) % 2
                panel = (r + q) % 8
                for s in range(SLOTS):
                    j = lcode[d, i * 2 + s]
                    m = place[panel * 4 + jnp.maximum(j, 0)]
                    c0 = jnp.where(j < 0, -3, rcode[m // 4, (m % 4) * 2])
                    c1 = jnp.where(j < 0, -3, rcode[m // 4, (m % 4) * 2 + 1])
                    for t in range(OUT):
                        o = ocode[i * 4 + t]
                        pick[(n * 2 + s) * 4 + t] = jnp.where(o == c0, 2 * m, jnp.where(o == c1, 2 * m + 1, ZERO))
        events.append((6.0, indices))
    if "y" in parts:
        arrived = []

        def pass_on(j):
            def run():
                a, b = relayed[j]
                a.wait_recv()
                p = remote(relay.at[rows(alpha[j])], left.at[4, rows(alpha[j])], north)
                b.wait_recv()
                m = remote(relay.at[rows(beta[j])], left.at[4, rows(beta[j])], south)
                arrived.append((p, m))
            return run

        def spread(j):
            def run():
                p, m = arrived[j]
                fs = []
                for copy, first in ((p, alpha[j]), (m, beta[j])):
                    copy.wait_recv()
                    if "x" in parts:
                        e = remote(left.at[4, rows(first)], left.at[7, rows(first)], east)
                        w = remote(left.at[4, rows(first)], left.at[5, rows(first)], west)
                        fs.append((first, e, w))
                later.append(fs)
            return run

        later = []

        def finish(j):
            def run():
                todo = []
                for first, e, w in later[j]:
                    if first in alpha:
                        e.wait_recv()
                        waits[6].append((first, remote(left.at[7, rows(first)], left.at[6, rows(first)], east)))
                        waits[5].append((first, w))
                    else:
                        w.wait_recv()
                        waits[6].append((first, remote(left.at[5, rows(first)], left.at[6, rows(first)], west)))
                        waits[7].append((first, e))
            return run

        for j in range(n):
            events.append((10.5 * (j + 1) / n, pass_on(j)))
            events.append((10.5 + 10.5 * (j + 1) / n, spread(j)))
            events.append((16 + 10.5 * (j + 1) / n, finish(j)))

    for _, run in sorted(events, key=lambda e: e[0]):
        run()

    own_left.wait()
    own_right.wait()
    right[ZERO] = jnp.zeros((BLOCK, BLOCK), jnp.bfloat16)
    for copy in right_waits:
        copy.wait_recv()
    for d in range(8):
        for _, copy in waits[d]:
            copy.wait_recv()

    if "compute" in parts:
        @pl.loop(0, ROWS)
        def _(i):
            lhs = jnp.concatenate([left[d, i, s] for d in range(8) for s in range(SLOTS)], axis=1)
            rhs = jnp.concatenate([
                jnp.concatenate([right[pick[((d * 8 + i) * 2 + s) * 4 + t]] for t in range(OUT)], axis=1)
                for d in range(8) for s in range(SLOTS)], axis=0)
            total = jnp.dot(lhs, rhs, preferred_element_type=jnp.float32).astype(jnp.bfloat16)
            for t in range(OUT):
                stage[i, t] = total[:, t * BLOCK:(t + 1) * BLOCK]
    done = pltpu.make_async_copy(stage, out_hbm, out_sem)
    done.start()
    for copy in sent:
        copy.wait_send()
    done.wait()


def slot_of(d):
    return d


def slot_of_row(d):
    dz, dc = d // 2, d % 2
    return ((4 - dz) % 4) * 2 + dc


def solution(mesh, parts=PARTS):
    def slot_of_q(d):
        return (d // 4) * 4 + (4 - d % 4) % 4

    globals()["slot_of"] = slot_of_q

    def step(*args):
        smem, hbm = pl.BlockSpec(memory_space=pltpu.SMEM), pl.BlockSpec(memory_space=pl.ANY)
        return pl.pallas_call(
            functools.partial(kernel, parts),
            out_shape=jax.ShapeDtypeStruct((ROWS, OUT, BLOCK, BLOCK), jnp.bfloat16),
            in_specs=[hbm, smem, smem, hbm, smem, smem, smem, smem, smem],
            out_specs=hbm,
            scratch_shapes=[
                pltpu.VMEM((8, ROWS, SLOTS, BLOCK, BLOCK), jnp.bfloat16),
                pltpu.VMEM((ROWS, SLOTS, BLOCK, BLOCK), jnp.bfloat16),
                pltpu.VMEM((65, BLOCK, BLOCK), jnp.bfloat16),
                pltpu.VMEM((ROWS, BLOCK, OUT * BLOCK), jnp.float32),
                pltpu.VMEM((ROWS, OUT, BLOCK, BLOCK), jnp.bfloat16),
                pltpu.SMEM((8, 128), jnp.int32),
                pltpu.SMEM((8, 128), jnp.int32),
                pltpu.SMEM((32,), jnp.int32),
                pltpu.SMEM((32,), jnp.int32),
                pltpu.SMEM((512,), jnp.int32),
                pltpu.SemaphoreType.DMA((N_COPIES,)),
                pltpu.SemaphoreType.DMA((N_COPIES,)),
                pltpu.SemaphoreType.DMA((2,)),
                pltpu.SemaphoreType.DMA,
            ],
            compiler_params=pltpu.CompilerParams(
                collective_id=0, has_side_effects=True, vmem_limit_bytes=48 * 1024 * 1024
            ),
        )(args[0], args[1], args[2], args[3].reshape(8, BLOCK, BLOCK), *args[4:])

    whole = P("row", "col", None, None)
    flat = P("row", "col")
    return jax.shard_map(
        step, mesh=mesh, in_specs=(whole, flat, flat, whole, flat, flat, flat, flat, P()),
        out_specs=whole, check_vma=False,
    )
```

```python
import functools

import jax
import jax.numpy as jnp
from jax import lax
from jax.experimental import pallas as pl
from jax.experimental.pallas import tpu as pltpu
from jax.sharding import PartitionSpec as P

MESH = pl.DeviceIdType.MESH
ROWS, SLOTS, OUT, PANEL, BLOCK = 8, 2, 4, 4, 128
HALF = ROWS // 2
GROUP = 9
N_COPIES = 136
PARTS = ("x", "y", "z", "compute")


def kernel(
    parts,
    left_hbm, lcol_hbm, lcount_hbm, right_hbm, rcol_hbm, rcount_hbm, ocol_hbm, ocount_hbm, owner_hbm,
    out_hbm,
    left, relay, right, acc, stage,
    lcol, lcount, rcol, rcount, ocol, ocount, owner,
    lcode, rcode, ocode, place_vmem, place,
    send_sem, recv_sem, local_sem, small_sem, out_sem, ready,
):
    r = lax.axis_index("row")
    c = lax.axis_index("col")
    z, core = r // 2, r % 2
    x, y, low = c // 24, (c // 3) % 8, c % 3

    def at_q(dx, dy):
        return (r, ((x + dx) % 4) * 24 + ((y + dy) % 8) * 3 + low)

    def at_row(dz, dcore):
        return (((z + dz) % 4) * 2 + (core + dcore) % 2, c)

    east, west, north, south = at_q(1, 0), at_q(3, 0), at_q(0, 2), at_q(0, 6)
    up, down, twin = at_row(1, 0), at_row(3, 0), at_row(0, 1)

    barrier = pltpu.get_barrier_semaphore()

    def greet(device):
        pl.semaphore_signal(barrier, inc=1, device_id=device, device_id_type=MESH)

    for device in (east, west, north, south, twin):
        greet(device)
    pl.when(z != 3)(lambda: greet(up))
    pl.when(z == 0)(lambda: greet(down))
    own_left = pltpu.make_async_copy(left_hbm, left.at[0], local_sem.at[0])
    own_left.start()
    own_right = pltpu.make_async_copy(right_hbm, right.at[pl.ds(0, 8)], local_sem.at[1])
    own_right.start()
    small = [
        pltpu.make_async_copy(src, dst, small_sem.at[n])
        for n, (src, dst) in enumerate((
            (lcol_hbm, lcol), (lcount_hbm, lcount), (rcol_hbm, rcol), (rcount_hbm, rcount),
            (ocol_hbm, ocol), (ocount_hbm, ocount), (owner_hbm, owner)))
    ]
    for copy in small:
        copy.start()
    pl.semaphore_wait(barrier, 5 + jnp.where(z != 0, 1, 0) + jnp.where(z == 3, 1, 0))
    pl.when(z != 0)(lambda: pl.semaphore_signal(ready.at[0], inc=1, device_id=down, device_id_type=MESH))
    pl.when(z == 3)(lambda: pl.semaphore_signal(ready.at[1], inc=1, device_id=up, device_id_type=MESH))

    sent = []

    def remote(src, dst, device, start=True):
        n = len(sent)
        copy = pltpu.make_async_remote_copy(
            src_ref=src, dst_ref=dst, send_sem=send_sem.at[n], recv_sem=recv_sem.at[n],
            device_id=device, device_id_type=MESH,
        )
        if start:
            copy.start()
        sent.append(copy)
        return copy

    def row(ref, i):
        return ref.at[pl.ds(i, 1)]

    def rslot(dz, dc, k):
        return right.at[pl.ds((dz * 2 + dc) * GROUP + k * 2, 2)]

    events = []
    pending = {}

    def need(d, i, copy):
        pending.setdefault((d, i), []).append(copy)

    def at(when):
        return lambda run: events.append((when, len(events), run))

    order_e = list(range(ROWS))
    order_w = list(range(HALF, ROWS)) + list(range(HALF))
    alpha, beta = order_e[:HALF], order_e[HALF:]
    if "y" in parts:
        to_n = [remote(row(left_hbm, i), row(relay, i), north) for i in alpha]
        to_s = [remote(row(left_hbm, i), row(relay, i), south) for i in beta]
    if "x" in parts:
        to_e, to_w = {}, {}
        for a, b in zip(order_e, order_w):
            to_e[a] = remote(row(left_hbm, a), left.at[3, pl.ds(a, 1)], east)
            to_w[b] = remote(row(left_hbm, b), left.at[1, pl.ds(b, 1)], west)
    if "z" in parts:
        to_up = [remote(right_hbm.at[pl.ds(2 * k, 2)], rslot(3, 0, k), up, False) for k in (0, 1, 2, 3)]
        to_down = [remote(right_hbm.at[pl.ds(2 * k, 2)], rslot(1, 0, k), down, False) for k in (2, 3, 0, 1)]

        def start(copies):
            for copy in copies:
                copy.start()

        def start_late(copies, n):
            pl.semaphore_wait(ready.at[n], 1)
            start(copies)

        pl.when(z == 3)(lambda: start(to_up))
        pl.when(z != 0)(lambda: start(to_down))
        to_twin = remote(right_hbm, right.at[pl.ds(GROUP, 8)], twin)

    for copy in small:
        copy.wait()
    panel = (r + x * 2 + y // 4) % 8
    for i in range(ROWS):
        for s in range(SLOTS):
            lcode[0, i * 2 + s] = jnp.where(s < lcount[0, i], panel * 4 + lcol[s, i], 32)
        for t in range(OUT):
            ocode[i * 4 + t] = jnp.where(t < ocount[0, i], ocol[t, i], 8)
    for k in range(PANEL):
        c0 = jnp.where(0 < rcount[0, k], rcol[0, k], -1)
        c1 = jnp.where(1 < rcount[0, k], rcol[1, k], -1)
        for n in range(8):
            rcode[0, k * 16 + n] = jnp.where(c0 == n, k * 2, jnp.where(c1 == n, k * 2 + 1, 8))
        rcode[0, k * 16 + 8] = 8
    for n in range(9):
        rcode[0, PANEL * 16 + n] = 8
    if "x" in parts:
        code_e = remote(lcode.at[0], lcode.at[3], east)
        code_w = remote(lcode.at[0], lcode.at[1], west)
    if "y" in parts:
        code_n = remote(lcode.at[0], lcode.at[8], north)
    if "z" in parts:
        code_up = remote(rcode.at[0], rcode.at[6], up, False)
        code_down = remote(rcode.at[0], rcode.at[2], down, False)
        to_up.append(code_up)
        to_down.append(code_down)
        pl.when(z == 3)(code_up.start)
        pl.when(z != 0)(code_down.start)
        code_twin = remote(rcode.at[0], rcode.at[1], twin)
    region = (y % 4) * 3 + low
    lane = lax.broadcasted_iota(jnp.int32, (1, 128), 1)
    owners = jnp.full((1, 128), 0, jnp.int32)
    for e in range(32):
        owners = jnp.where(lane == e, owner[region, e], owners)
    rank = jnp.zeros((1, 128), jnp.int32)
    for e in range(32):
        rank += jnp.where((owners == owner[region, e]) & (lane > e), 1, 0)
    rank = jnp.minimum(rank, 3)
    slot = (((owners >> 1) - z) & 3) * 2 + ((owners + core) & 1)
    place_vmem[pl.ds(0, 1), :] = jnp.where(lane < 32, slot, 0)
    place_vmem[pl.ds(1, 1), :] = jnp.where(lane < 32, rank, 4) * 16
    placed = pltpu.make_async_copy(place_vmem, place, local_sem.at[2])
    placed.start()
    for n in range(8):
        right[pl.ds(n * GROUP + 8, 1)] = jnp.zeros((1, BLOCK, BLOCK), jnp.bfloat16)

    def ring(d, i, e, w, when):
        @at(when)
        def _():
            if i in alpha:
                e.wait_recv()
                need(d + 2, i, remote(left.at[d + 3, pl.ds(i, 1)], left.at[d + 2, pl.ds(i, 1)], east))
                need(d + 1, i, w)
            else:
                w.wait_recv()
                need(d + 2, i, remote(left.at[d + 1, pl.ds(i, 1)], left.at[d + 2, pl.ds(i, 1)], west))
                need(d + 3, i, e)

    codes = []
    if "x" in parts:
        for j in range(HALF):
            ring(0, alpha[j], to_e[alpha[j]], to_w[alpha[j]], 3 + 1.5 * j)
            ring(0, beta[j], to_e[beta[j]], to_w[beta[j]], 3 + 1.5 * j)

        @at(7.6)
        def _():
            code_e.wait_recv()
            codes.extend([remote(lcode.at[3], lcode.at[2], east), code_w])
    if "y" in parts:
        crossed = {}

        def crossing(j):
            @at(5 + 2.7 * j)
            def _():
                to_n[j].wait_recv()
                crossed[alpha[j]] = remote(row(relay, alpha[j]), left.at[4, pl.ds(alpha[j], 1)], north)
                to_s[j].wait_recv()
                crossed[beta[j]] = remote(row(relay, beta[j]), left.at[4, pl.ds(beta[j], 1)], south)
                if j == HALF - 1:
                    code_n.wait_recv()
                    crossed["code"] = remote(lcode.at[8], lcode.at[4], north)

            @at(14.5 + 2.7 * j)
            def _():
                for i in (alpha[j], beta[j]):
                    crossed[i].wait_recv()
                    if "x" not in parts:
                        continue
                    e = remote(left.at[4, pl.ds(i, 1)], left.at[7, pl.ds(i, 1)], east)
                    w = remote(left.at[4, pl.ds(i, 1)], left.at[5, pl.ds(i, 1)], west)
                    passed[i] = (e, w)
                if j == HALF - 1:
                    crossed["code"].wait_recv()
                    if "x" in parts:
                        passed["code"] = (
                            remote(lcode.at[4], lcode.at[7], east), remote(lcode.at[4], lcode.at[5], west))

            @at(20 + 3.5 * j)
            def _():
                if "x" not in parts:
                    return
                for i in (alpha[j], beta[j]):
                    e, w = passed[i]
                    if i in alpha:
                        e.wait_recv()
                        need(6, i, remote(left.at[7, pl.ds(i, 1)], left.at[6, pl.ds(i, 1)], east))
                        need(5, i, w)
                    else:
                        w.wait_recv()
                        need(6, i, remote(left.at[5, pl.ds(i, 1)], left.at[6, pl.ds(i, 1)], west))
                        need(7, i, e)
                if j == HALF - 1:
                    e, w = passed["code"]
                    e.wait_recv()
                    codes.extend([remote(lcode.at[7], lcode.at[6], east), w])

        passed = {}
        for j in range(HALF):
            crossing(j)

    if "z" in parts:
        at(4)(lambda: pl.when(z != 3)(lambda: start_late(to_up, 0)))
        at(9)(lambda: pl.when(z == 0)(lambda: start_late(to_down, 1)))
        over_up = [remote(rslot(3, 0, k), rslot(2, 0, k), up, False) for k in (0, 1)]
        over_down = [remote(rslot(1, 0, k), rslot(2, 0, k), down, False) for k in (2, 3)]
        over_code = remote(rcode.at[6], rcode.at[4], up, False)
        share_3 = [remote(rslot(3, 0, k), rslot(3, 1, k), twin, False) for k in (0, 1, 2, 3)]
        share_1 = [remote(rslot(1, 0, k), rslot(1, 1, k), twin, False) for k in (2, 3, 0, 1)]
        share_2 = [remote(rslot(2, 0, k), rslot(2, 1, k), twin, False) for k in (0, 1, 2, 3)]
        share_code = [remote(rcode.at[2 * d], rcode.at[2 * d + 1], twin, False) for d in (1, 2, 3)]

        def from_below(n):
            to_up[n].wait_recv()
            if n < 2:
                over_up[n].start()
            share_3[n].start()
            if n == 3:
                code_up.wait_recv()
                over_code.start()
                share_code[2].start()

        def from_above(n):
            to_down[n].wait_recv()
            if n < 2:
                over_down[n].start()
            share_1[n].start()
            if n == 3:
                code_down.wait_recv()
                share_code[0].start()

        for n in range(4):
            at(8.5 + 2.5 * n)(functools.partial(lambda n: pl.when(z != 0)(lambda: from_below(n)), n))
            at(19 + 2 * n)(functools.partial(lambda n: pl.when(z == 0)(lambda: from_below(n)), n))
            at(11 + 2.5 * n)(functools.partial(from_above, n))

        @at(27)
        def _():
            for n, copy in enumerate(over_up + over_down):
                copy.wait_recv()
                share_2[n].start()
            over_code.wait_recv()
            share_code[1].start()

        def right_done():
            own_right.wait()
            to_twin.wait_recv()
            code_twin.wait_recv()
            for copy in share_3 + share_1 + share_2 + share_code:
                copy.wait_recv()
            placed.wait()
    else:
        def right_done():
            own_right.wait()
            placed.wait()

    def product(i, ds):
        lhs = jnp.concatenate([left[d, i, s] for d in ds for s in range(SLOTS)], axis=1)
        rhs = []
        for d in ds:
            for s in range(SLOTS):
                k = lcode[d, i * 2 + s]
                where, first = place[0, k], place[1, k]
                rhs.append(jnp.concatenate([
                    right[where * GROUP + rcode[where, first + ocode[i * 4 + t]]] for t in range(OUT)], axis=1))
        return jnp.dot(lhs, jnp.concatenate(rhs, axis=0), preferred_element_type=jnp.float32)

    def settle(ds, rows):
        for d in ds:
            for i in rows:
                for copy in pending.pop((d, i), []):
                    copy.wait_recv()

    for _, _, run in sorted(events, key=lambda e: e[:2]):
        run()
    own_left.wait()
    right_done()
    for copy in codes:
        copy.wait_recv()
    settle(range(8), range(ROWS))
    if "compute" in parts:
        @pl.loop(0, ROWS)
        def _(i):
            total = product(i, range(8)).astype(jnp.bfloat16)
            for t in range(OUT):
                stage[i, t] = total[:, t * BLOCK:(t + 1) * BLOCK]
            pltpu.make_async_copy(stage.at[i], out_hbm.at[i], out_sem.at[i]).start()
        for i in range(ROWS):
            pltpu.make_async_copy(stage.at[i], out_hbm.at[i], out_sem.at[i]).wait()
    for copy in sent:
        copy.wait_send()


def solution(mesh, parts=PARTS):
    def step(*args):
        hbm = pl.BlockSpec(memory_space=pl.ANY)
        return pl.pallas_call(
            functools.partial(kernel, parts),
            out_shape=jax.ShapeDtypeStruct((ROWS, OUT, BLOCK, BLOCK), jnp.bfloat16),
            in_specs=[hbm] * 9,
            out_specs=hbm,
            scratch_shapes=[
                pltpu.VMEM((8, ROWS, SLOTS, BLOCK, BLOCK), jnp.bfloat16),
                pltpu.VMEM((ROWS, SLOTS, BLOCK, BLOCK), jnp.bfloat16),
                pltpu.VMEM((8 * GROUP, BLOCK, BLOCK), jnp.bfloat16),
                pltpu.VMEM((ROWS, BLOCK, OUT * BLOCK), jnp.float32),
                pltpu.VMEM((ROWS, OUT, BLOCK, BLOCK), jnp.bfloat16),
                pltpu.SMEM((SLOTS, ROWS), jnp.int32),
                pltpu.SMEM((1, ROWS), jnp.int32),
                pltpu.SMEM((2, PANEL), jnp.int32),
                pltpu.SMEM((1, PANEL), jnp.int32),
                pltpu.SMEM((OUT, ROWS), jnp.int32),
                pltpu.SMEM((1, ROWS), jnp.int32),
                pltpu.SMEM((12, 32), jnp.int32),
                pltpu.SMEM((9, 128), jnp.int32),
                pltpu.SMEM((8, 128), jnp.int32),
                pltpu.SMEM((32,), jnp.int32),
                pltpu.VMEM((2, 128), jnp.int32),
                pltpu.SMEM((2, 128), jnp.int32),
                pltpu.SemaphoreType.DMA((N_COPIES,)),
                pltpu.SemaphoreType.DMA((N_COPIES,)),
                pltpu.SemaphoreType.DMA((3,)),
                pltpu.SemaphoreType.DMA((7,)),
                pltpu.SemaphoreType.DMA((ROWS,)),
                pltpu.SemaphoreType.REGULAR((2,)),
            ],
            compiler_params=pltpu.CompilerParams(
                collective_id=0, has_side_effects=True, vmem_limit_bytes=58 * 1024 * 1024
            ),
        )(args[0], args[1].T, args[2].T, args[3].reshape(8, BLOCK, BLOCK), args[4].T, args[5].T, args[6].T,
          args[7].T, args[8])

    whole = P("row", "col", None, None)
    flat = P("row", "col")
    return jax.shard_map(
        step, mesh=mesh, in_specs=(whole, flat, flat, whole, flat, flat, flat, flat, P()),
        out_specs=whole, check_vma=False,
    )
```

```python
import functools

import jax
import jax.numpy as jnp
from jax import lax
from jax.experimental import pallas as pl
from jax.experimental.pallas import tpu as pltpu
from jax.sharding import PartitionSpec as P

MESH = pl.DeviceIdType.MESH
ROWS, SLOTS, OUT, PANEL, BLOCK = 8, 2, 4, 4, 128
HALF = ROWS // 2
GROUP = 9
N_COPIES = 136
PARTS = ("x", "y", "z", "compute")


def kernel(
    parts,
    left_hbm, lcol_hbm, lcount_hbm, right_hbm, rcol_hbm, rcount_hbm, ocol_hbm, ocount_hbm, owner_hbm,
    out_hbm,
    left, relay, right, acc, stage,
    lcol, lcount, rcol, rcount, ocol, ocount, owner,
    lcode, rcode, ocode, place_vmem, place, pick,
    send_sem, recv_sem, local_sem, small_sem, out_sem, ready,
):
    r = lax.axis_index("row")
    c = lax.axis_index("col")
    z, core = r // 2, r % 2
    x, y, low = c // 24, (c // 3) % 8, c % 3

    def at_q(dx, dy):
        return (r, ((x + dx) % 4) * 24 + ((y + dy) % 8) * 3 + low)

    def at_row(dz, dcore):
        return (((z + dz) % 4) * 2 + (core + dcore) % 2, c)

    east, west, north, south = at_q(1, 0), at_q(3, 0), at_q(0, 2), at_q(0, 6)
    up, down, twin = at_row(1, 0), at_row(3, 0), at_row(0, 1)

    def is_first(dx, dy, dz, dc):
        return (
            ((x + dx) % 4 == 0) & ((y + dy) % 8 == 0) & (low == 0) & ((z + dz) % 4 == 0) & ((core + dc) % 2 == 0))

    first = is_first(0, 0, 0, 0)
    turn = y // 2
    neighbours = [east, west, north, south, twin, up, down]
    opposite = [1, 0, 3, 2, 4, 6, 5]
    later = [
        ((x != 3) | is_first(1, 0, 0, 0)) & ~first,
        ((x == 0) | is_first(3, 0, 0, 0)) & ~first,
        ((turn <= 1) | is_first(0, 2, 0, 0)) & ~first,
        ((turn == 0) | (turn == 3) | is_first(0, 6, 0, 0)) & ~first,
        ((core == 1) | is_first(0, 0, 0, 1)) & ~first,
        (z != 3) & ~first,
        (z == 0) | is_first(0, 0, 3, 0),
    ]
    barrier = pltpu.get_barrier_semaphore()

    def greet(device):
        pl.semaphore_signal(barrier, inc=1, device_id=device, device_id_type=MESH)

    def answer(n):
        pl.semaphore_signal(ready.at[opposite[n]], inc=1, device_id=neighbours[n], device_id_type=MESH)

    for n, device in enumerate(neighbours):
        pl.when(later[n])(functools.partial(greet, device))
    own_left = pltpu.make_async_copy(left_hbm, left.at[0], local_sem.at[0])
    own_left.start()
    own_right = pltpu.make_async_copy(right_hbm, right.at[pl.ds(0, 8)], local_sem.at[1])
    own_right.start()
    small = [
        pltpu.make_async_copy(src, dst, small_sem.at[n])
        for n, (src, dst) in enumerate((
            (lcol_hbm, lcol), (lcount_hbm, lcount), (rcol_hbm, rcol), (rcount_hbm, rcount),
            (ocol_hbm, ocol), (ocount_hbm, ocount), (owner_hbm, owner)))
    ]
    for copy in small:
        copy.start()
    earlier = sum(jnp.where(l, 0, 1) for l in later)
    pl.when(earlier > 0)(lambda: pl.semaphore_wait(barrier, earlier))
    for n in range(7):
        pl.when(~later[n])(functools.partial(answer, n))

    for copy in small:
        copy.wait()
    panel = (r + x * 2 + y // 4) % 8
    for i in range(ROWS):
        for s in range(SLOTS):
            lcode[0, i * 2 + s] = jnp.where(s < lcount[0, i], panel * 4 + lcol[s, i], 32)
        for t in range(OUT):
            ocode[i * 4 + t] = jnp.where(t < ocount[0, i], ocol[t, i], 8)
    for k in range(PANEL):
        c0 = jnp.where(0 < rcount[0, k], rcol[0, k], -1)
        c1 = jnp.where(1 < rcount[0, k], rcol[1, k], -1)
        for n in range(8):
            rcode[0, k * 16 + n] = jnp.where(c0 == n, k * 2, jnp.where(c1 == n, k * 2 + 1, 8))
        rcode[0, k * 16 + 8] = 8
    for n in range(9):
        rcode[0, PANEL * 16 + n] = 8
    sent = []

    def remote(src, dst, device, start=True):
        n = len(sent)
        copy = pltpu.make_async_remote_copy(
            src_ref=src, dst_ref=dst, send_sem=send_sem.at[n], recv_sem=recv_sem.at[n],
            device_id=device, device_id_type=MESH,
        )
        if start:
            copy.start()
        sent.append(copy)
        return copy

    def row(ref, i):
        return ref.at[pl.ds(i, 1)]

    def rslot(dz, dc, k):
        return right.at[pl.ds((dz * 2 + dc) * GROUP + k * 2, 2)]

    events = []
    pending = {}

    def need(d, i, copy):
        pending.setdefault((d, i), []).append(copy)

    def at(when):
        return lambda run: events.append((when, len(events), run))

    order_e = list(range(ROWS))
    order_w = list(range(HALF, ROWS)) + list(range(HALF))
    alpha, beta = order_e[:HALF], order_e[HALF:]
    code_up = remote(rcode.at[0], rcode.at[6], up, False)
    code_down = remote(rcode.at[0], rcode.at[2], down, False)
    code_twin = remote(rcode.at[0], rcode.at[1], twin, False)
    code_e = remote(lcode.at[0], lcode.at[3], east, False)
    code_w = remote(lcode.at[0], lcode.at[1], west, False)
    code_n = remote(lcode.at[0], lcode.at[8], north, False)
    to_up = [remote(right_hbm.at[pl.ds(2 * k, 2)], rslot(3, 0, k), up, False) for k in (0, 1, 2, 3)]
    to_down = [remote(right_hbm.at[pl.ds(2 * k, 2)], rslot(1, 0, k), down, False) for k in (2, 3, 0, 1)]
    to_e = {i: remote(row(left_hbm, i), left.at[3, pl.ds(i, 1)], east, False) for i in order_e}
    to_w = {i: remote(row(left_hbm, i), left.at[1, pl.ds(i, 1)], west, False) for i in order_w}
    to_n = [remote(row(left_hbm, i), row(relay, i), north, False) for i in alpha]
    to_s = [remote(row(left_hbm, i), row(relay, i), south, False) for i in beta]
    to_twin = remote(right_hbm, right.at[pl.ds(GROUP, 8)], twin, False)
    groups = [
        [code_e] + list(to_e.values()), [code_w] + list(to_w.values()), [code_n] + to_n, to_s,
        [code_twin, to_twin], [code_up] + to_up, [code_down] + to_down]

    def start(copies):
        for copy in copies:
            copy.start()

    def start_late(n):
        pl.semaphore_wait(ready.at[n], 1)
        start(groups[n])

    for n in (5, 6, 0, 1, 2, 3, 4):
        pl.when(~later[n])(functools.partial(start, groups[n]))
    for n in (0, 1, 2, 3, 4):
        pl.when(later[n])(functools.partial(start_late, n))

    region = (y % 4) * 3 + low
    lane = lax.broadcasted_iota(jnp.int32, (1, 128), 1)
    owners = jnp.full((1, 128), 0, jnp.int32)
    for e in range(32):
        owners = jnp.where(lane == e, owner[region, e], owners)
    rank = jnp.zeros((1, 128), jnp.int32)
    for e in range(32):
        rank += jnp.where((owners == owner[region, e]) & (lane > e), 1, 0)
    rank = jnp.minimum(rank, 3)
    slot = (((owners >> 1) - z) & 3) * 2 + ((owners + core) & 1)
    place_vmem[pl.ds(0, 1), :] = jnp.where(lane < 32, slot, 0)
    place_vmem[pl.ds(1, 1), :] = jnp.where(lane < 32, rank, 4) * 16
    placed = pltpu.make_async_copy(place_vmem, place, local_sem.at[2])
    placed.start()
    for n in range(8):
        right[pl.ds(n * GROUP + 8, 1)] = jnp.zeros((1, BLOCK, BLOCK), jnp.bfloat16)

    def ring(d, i, e, w, when):
        @at(when)
        def _():
            if i in alpha:
                e.wait_recv()
                need(d + 2, i, remote(left.at[d + 3, pl.ds(i, 1)], left.at[d + 2, pl.ds(i, 1)], east))
                need(d + 1, i, w)
            else:
                w.wait_recv()
                need(d + 2, i, remote(left.at[d + 1, pl.ds(i, 1)], left.at[d + 2, pl.ds(i, 1)], west))
                need(d + 3, i, e)

    codes = []
    if "x" in parts:
        for j in range(HALF):
            ring(0, alpha[j], to_e[alpha[j]], to_w[alpha[j]], 3 + 1.5 * j)
            ring(0, beta[j], to_e[beta[j]], to_w[beta[j]], 3 + 1.5 * j)

        @at(7.6)
        def _():
            code_e.wait_recv()
            codes.extend([remote(lcode.at[3], lcode.at[2], east), code_w])
    if "y" in parts:
        crossed = {}

        def crossing(j):
            @at(5 + 2.7 * j)
            def _():
                to_n[j].wait_recv()
                crossed[alpha[j]] = remote(row(relay, alpha[j]), left.at[4, pl.ds(alpha[j], 1)], north)
                to_s[j].wait_recv()
                crossed[beta[j]] = remote(row(relay, beta[j]), left.at[4, pl.ds(beta[j], 1)], south)
                if j == 0:
                    code_n.wait_recv()
                    crossed["code"] = remote(lcode.at[8], lcode.at[4], north)

            @at(14.5 + 2.7 * j)
            def _():
                for i in (alpha[j], beta[j]):
                    crossed[i].wait_recv()
                    if "x" not in parts:
                        continue
                    e = remote(left.at[4, pl.ds(i, 1)], left.at[7, pl.ds(i, 1)], east)
                    w = remote(left.at[4, pl.ds(i, 1)], left.at[5, pl.ds(i, 1)], west)
                    passed[i] = (e, w)
                if j == 0:
                    crossed["code"].wait_recv()
                    if "x" in parts:
                        passed["code"] = (
                            remote(lcode.at[4], lcode.at[7], east), remote(lcode.at[4], lcode.at[5], west))

            @at(20 + 3.5 * j)
            def _():
                if "x" not in parts:
                    return
                for i in (alpha[j], beta[j]):
                    e, w = passed[i]
                    if i in alpha:
                        e.wait_recv()
                        need(6, i, remote(left.at[7, pl.ds(i, 1)], left.at[6, pl.ds(i, 1)], east))
                        need(5, i, w)
                    else:
                        w.wait_recv()
                        need(6, i, remote(left.at[5, pl.ds(i, 1)], left.at[6, pl.ds(i, 1)], west))
                        need(7, i, e)
                if j == 0:
                    e, w = passed["code"]
                    e.wait_recv()
                    codes.extend([remote(lcode.at[7], lcode.at[6], east), w])

        passed = {}
        for j in range(HALF):
            crossing(j)

    if "z" in parts:
        at(4)(lambda: pl.when(later[5])(lambda: start_late(5)))
        at(9)(lambda: pl.when(later[6])(lambda: start_late(6)))
        over_up = [remote(rslot(3, 0, k), rslot(2, 0, k), up, False) for k in (0, 1)]
        over_down = [remote(rslot(1, 0, k), rslot(2, 0, k), down, False) for k in (2, 3)]
        over_code = remote(rcode.at[6], rcode.at[4], up, False)
        share_3 = [remote(rslot(3, 0, k), rslot(3, 1, k), twin, False) for k in (0, 1, 2, 3)]
        share_1 = [remote(rslot(1, 0, k), rslot(1, 1, k), twin, False) for k in (2, 3, 0, 1)]
        share_2 = [remote(rslot(2, 0, k), rslot(2, 1, k), twin, False) for k in (0, 1, 2, 3)]
        share_code = [remote(rcode.at[2 * d], rcode.at[2 * d + 1], twin, False) for d in (1, 2, 3)]

        def from_below(n):
            if n == 0:
                code_up.wait_recv()
                over_code.start()
                share_code[2].start()
            to_up[n].wait_recv()
            if n < 2:
                over_up[n].start()
            share_3[n].start()

        def from_above(n):
            if n == 0:
                code_down.wait_recv()
                share_code[0].start()
            to_down[n].wait_recv()
            if n < 2:
                over_down[n].start()
            share_1[n].start()

        def code_over():
            over_code.wait_recv()
            share_code[1].start()

        def from_across():
            for n, copy in enumerate(over_up + over_down):
                copy.wait_recv()
                share_2[n].start()

        for n in range(4):
            at((10, 16, 24, 27.2)[n])(functools.partial(lambda n: pl.when(z != 0)(lambda: from_below(n)), n))
            at((20, 25, 31.5, 31.6)[n])(functools.partial(lambda n: pl.when(z == 0)(lambda: from_below(n)), n))
            at((10.5, 16.5, 24, 27.2)[n])(functools.partial(from_above, n))
        at(20.5)(code_over)
        at(31.8)(from_across)

        def codes_done():
            code_twin.wait_recv()
            for copy in share_code + codes:
                copy.wait_recv()
            placed.wait()

        def right_done():
            own_right.wait()
            to_twin.wait_recv()
            for copy in share_3 + share_1 + share_2:
                copy.wait_recv()
    else:
        def right_done():
            pl.when(z != 3)(lambda: pl.semaphore_wait(ready.at[0], 1))
            pl.when(z == 0)(lambda: pl.semaphore_wait(ready.at[1], 1))
            own_right.wait()

        def codes_done():
            for copy in codes:
                copy.wait_recv()
            placed.wait()

    def picks(first):
        if first == 0:
            codes_done()

        @pl.loop(first, first + HALF)
        def _(i):
            for d in range(8):
                for s in range(SLOTS):
                    k = lcode[d, i * 2 + s]
                    where, at = place[0, k], place[1, k]
                    for t in range(OUT):
                        pick[i * 64 + (d * 2 + s) * 4 + t] = where * GROUP + rcode[where, at + ocode[i * 4 + t]]

    events.append((23.7, 900, lambda: picks(0)))
    events.append((27.1, 901, lambda: picks(HALF)))

    def product(i, ds, half):
        total = jnp.zeros((BLOCK, 2 * BLOCK), jnp.float32)
        for d in ds:
            lhs = jnp.concatenate([left[d, i, s] for s in range(SLOTS)], axis=1)
            rhs = jnp.concatenate([
                jnp.concatenate([right[pick[i * 64 + (d * 2 + s) * 4 + half * 2 + t]] for t in range(2)], axis=1)
                for s in range(SLOTS)], axis=0)
            total += jnp.dot(lhs, rhs, preferred_element_type=jnp.float32)
        return total

    def settle(ds, rows):
        for d in ds:
            for i in rows:
                for copy in pending.pop((d, i), []):
                    copy.wait_recv()

    for _, _, run in sorted(events, key=lambda e: e[:2]):
        run()
    own_left.wait()
    right_done()
    settle(range(4), range(ROWS))
    if "compute" in parts:
        @pl.loop(0, ROWS)
        def _(i):
            for half in range(2):
                acc[i, half] = product(i, range(4), half)
    for j in range(HALF):
        settle(range(4, 8), (j, j + HALF))
        if "compute" in parts:
            @pl.loop(0, 2)
            def _(h):
                i = j + h * HALF
                for half in range(2):
                    total = (acc[i, half] + product(i, range(4, 8), half)).astype(jnp.bfloat16)
                    for t in range(2):
                        stage[i, half * 2 + t] = total[:, t * BLOCK:(t + 1) * BLOCK]
                pltpu.make_async_copy(stage.at[i], out_hbm.at[i], out_sem.at[i]).start()
    if "compute" in parts:
        for i in range(ROWS):
            pltpu.make_async_copy(stage.at[i], out_hbm.at[i], out_sem.at[i]).wait()
    for copy in sent:
        copy.wait_send()


def solution(mesh, parts=PARTS):
    def step(*args):
        hbm = pl.BlockSpec(memory_space=pl.ANY)
        return pl.pallas_call(
            functools.partial(kernel, parts),
            out_shape=jax.ShapeDtypeStruct((ROWS, OUT, BLOCK, BLOCK), jnp.bfloat16),
            in_specs=[hbm] * 9,
            out_specs=hbm,
            scratch_shapes=[
                pltpu.VMEM((8, ROWS, SLOTS, BLOCK, BLOCK), jnp.bfloat16),
                pltpu.VMEM((ROWS, SLOTS, BLOCK, BLOCK), jnp.bfloat16),
                pltpu.VMEM((8 * GROUP, BLOCK, BLOCK), jnp.bfloat16),
                pltpu.VMEM((ROWS, 2, BLOCK, 2 * BLOCK), jnp.float32),
                pltpu.VMEM((ROWS, OUT, BLOCK, BLOCK), jnp.bfloat16),
                pltpu.SMEM((SLOTS, ROWS), jnp.int32),
                pltpu.SMEM((1, ROWS), jnp.int32),
                pltpu.SMEM((2, PANEL), jnp.int32),
                pltpu.SMEM((1, PANEL), jnp.int32),
                pltpu.SMEM((OUT, ROWS), jnp.int32),
                pltpu.SMEM((1, ROWS), jnp.int32),
                pltpu.SMEM((12, 32), jnp.int32),
                pltpu.SMEM((9, 128), jnp.int32),
                pltpu.SMEM((8, 128), jnp.int32),
                pltpu.SMEM((32,), jnp.int32),
                pltpu.VMEM((2, 128), jnp.int32),
                pltpu.SMEM((2, 128), jnp.int32),
                pltpu.SMEM((512,), jnp.int32),
                pltpu.SemaphoreType.DMA((N_COPIES,)),
                pltpu.SemaphoreType.DMA((N_COPIES,)),
                pltpu.SemaphoreType.DMA((3,)),
                pltpu.SemaphoreType.DMA((7,)),
                pltpu.SemaphoreType.DMA((ROWS,)),
                pltpu.SemaphoreType.REGULAR((7,)),
            ],
            compiler_params=pltpu.CompilerParams(
                collective_id=0, has_side_effects=True, vmem_limit_bytes=58 * 1024 * 1024
            ),
        )(args[0], args[1].T, args[2].T, args[3].reshape(8, BLOCK, BLOCK), args[4].T, args[5].T, args[6].T,
          args[7].T, args[8])

    whole = P("row", "col", None, None)
    flat = P("row", "col")
    return jax.shard_map(
        step, mesh=mesh, in_specs=(whole, flat, flat, whole, flat, flat, flat, flat, P()),
        out_specs=whole, check_vma=False,
    )
```

```python
import functools

import jax
import jax.numpy as jnp
from jax import lax
from jax.experimental import pallas as pl
from jax.experimental.pallas import tpu as pltpu
from jax.sharding import PartitionSpec as P

MESH = pl.DeviceIdType.MESH
ROWS, SLOTS, OUT, PANEL, BLOCK = 8, 2, 4, 4, 128
HALF = ROWS // 2
GROUP = 9
N_COPIES = 136
PARTS = ("x", "y", "z", "compute")


def kernel(
    parts,
    left_hbm, lcol_hbm, lcount_hbm, right_hbm, rcol_hbm, rcount_hbm, ocol_hbm, ocount_hbm, owner_hbm,
    out_hbm,
    left, relay, right, acc, stage,
    lcol, lcount, rcol, rcount, ocol, ocount, owner,
    lcode, rcode, ocode, place_vmem, place, pick,
    send_sem, recv_sem, local_sem, small_sem, out_sem, ready,
):
    r = lax.axis_index("row")
    c = lax.axis_index("col")
    z, core = r // 2, r % 2
    x, y, low = c // 24, (c // 3) % 8, c % 3

    def at_q(dx, dy):
        return (r, ((x + dx) % 4) * 24 + ((y + dy) % 8) * 3 + low)

    def at_row(dz, dcore):
        return (((z + dz) % 4) * 2 + (core + dcore) % 2, c)

    east, west, north, south = at_q(1, 0), at_q(3, 0), at_q(0, 2), at_q(0, 6)
    up, down, twin = at_row(1, 0), at_row(3, 0), at_row(0, 1)

    def is_first(dx, dy, dz, dc):
        return (
            ((x + dx) % 4 == 0) & ((y + dy) % 8 == 0) & (low == 0) & ((z + dz) % 4 == 0) & ((core + dc) % 2 == 0))

    first = is_first(0, 0, 0, 0)
    turn = y // 2
    neighbours = [east, west, north, south, twin, up, down]
    opposite = [1, 0, 3, 2, 4, 6, 5]
    later = [
        ((x != 3) | is_first(1, 0, 0, 0)) & ~first,
        ((x == 0) | is_first(3, 0, 0, 0)) & ~first,
        ((turn <= 1) | is_first(0, 2, 0, 0)) & ~first,
        ((turn == 0) | (turn == 3) | is_first(0, 6, 0, 0)) & ~first,
        ((core == 1) | is_first(0, 0, 0, 1)) & ~first,
        (z != 3) & ~first,
        (z == 0) | is_first(0, 0, 3, 0),
    ]
    barrier = pltpu.get_barrier_semaphore()

    def greet(device):
        pl.semaphore_signal(barrier, inc=1, device_id=device, device_id_type=MESH)

    def answer(n):
        pl.semaphore_signal(ready.at[opposite[n]], inc=1, device_id=neighbours[n], device_id_type=MESH)

    for n, device in enumerate(neighbours):
        pl.when(later[n])(functools.partial(greet, device))
    own_left = pltpu.make_async_copy(left_hbm, left.at[0], local_sem.at[0])
    own_left.start()
    own_right = pltpu.make_async_copy(right_hbm, right.at[pl.ds(0, 8)], local_sem.at[1])
    own_right.start()
    small = [
        pltpu.make_async_copy(src, dst, small_sem.at[n])
        for n, (src, dst) in enumerate((
            (lcol_hbm, lcol), (lcount_hbm, lcount), (rcol_hbm, rcol), (rcount_hbm, rcount),
            (ocol_hbm, ocol), (ocount_hbm, ocount), (owner_hbm, owner)))
    ]
    for copy in small:
        copy.start()
    earlier = sum(jnp.where(l, 0, 1) for l in later)
    pl.when(earlier > 0)(lambda: pl.semaphore_wait(barrier, earlier))
    for n in range(7):
        pl.when(~later[n])(functools.partial(answer, n))

    sent = []

    def remote(src, dst, device, start=True):
        n = len(sent)
        copy = pltpu.make_async_remote_copy(
            src_ref=src, dst_ref=dst, send_sem=send_sem.at[n], recv_sem=recv_sem.at[n],
            device_id=device, device_id_type=MESH,
        )
        if start:
            copy.start()
        sent.append(copy)
        return copy

    def row(ref, i):
        return ref.at[pl.ds(i, 1)]

    def rslot(dz, dc, k):
        return right.at[pl.ds((dz * 2 + dc) * GROUP + k * 2, 2)]

    events = []
    pending = {}

    def need(d, i, copy):
        pending.setdefault((d, i), []).append(copy)

    def at(when):
        return lambda run: events.append((when, len(events), run))

    order_e = list(range(ROWS))
    order_w = list(range(HALF, ROWS)) + list(range(HALF))
    alpha, beta = order_e[:HALF], order_e[HALF:]
    code_up = remote(rcode.at[0], rcode.at[6], up, False)
    code_down = remote(rcode.at[0], rcode.at[2], down, False)
    code_twin = remote(rcode.at[0], rcode.at[1], twin, False)
    code_e = remote(lcode.at[0], lcode.at[3], east, False)
    code_w = remote(lcode.at[0], lcode.at[1], west, False)
    code_n = remote(lcode.at[0], lcode.at[8], north, False)
    to_up = [remote(right_hbm.at[pl.ds(2 * k, 2)], rslot(3, 0, k), up, False) for k in (0, 1, 2, 3)]
    to_down = [remote(right_hbm.at[pl.ds(2 * k, 2)], rslot(1, 0, k), down, False) for k in (2, 3, 0, 1)]
    to_e = {i: remote(row(left_hbm, i), left.at[3, pl.ds(i, 1)], east, False) for i in order_e}
    to_w = {i: remote(row(left_hbm, i), left.at[1, pl.ds(i, 1)], west, False) for i in order_w}
    to_n = [remote(row(left_hbm, i), row(relay, i), north, False) for i in alpha]
    to_s = [remote(row(left_hbm, i), row(relay, i), south, False) for i in beta]
    to_twin = remote(right_hbm, right.at[pl.ds(GROUP, 8)], twin, False)
    east_rows, west_rows = list(to_e.values()), list(to_w.values())
    heads = [east_rows[:1], west_rows[:1], [], [], [], to_up[:0], to_down[:0]]
    tails = [
        [code_e] + east_rows[1:], [code_w] + west_rows[1:], [code_n] + to_n, to_s,
        [code_twin, to_twin], [code_up] + to_up[0:], [code_down] + to_down[0:]]

    def start(copies):
        for copy in copies:
            copy.start()

    def start_late(n):
        pl.semaphore_wait(ready.at[n], 1)
        start(heads[n] + tails[n])

    for n in (5, 6, 0, 1):
        pl.when(~later[n])(functools.partial(start, heads[n]))
    for copy in small:
        copy.wait()
    panel = (r + x * 2 + y // 4) % 8
    for i in range(ROWS):
        for s in range(SLOTS):
            lcode[0, i * 2 + s] = jnp.where(s < lcount[0, i], panel * 4 + lcol[s, i], 32)
        for t in range(OUT):
            ocode[i * 4 + t] = jnp.where(t < ocount[0, i], ocol[t, i], 8)
    for k in range(PANEL):
        c0 = jnp.where(0 < rcount[0, k], rcol[0, k], -1)
        c1 = jnp.where(1 < rcount[0, k], rcol[1, k], -1)
        for n in range(8):
            rcode[0, k * 16 + n] = jnp.where(c0 == n, k * 2, jnp.where(c1 == n, k * 2 + 1, 8))
        rcode[0, k * 16 + 8] = 8
    for n in range(9):
        rcode[0, PANEL * 16 + n] = 8
    for n in (5, 6, 0, 1, 2, 3, 4):
        pl.when(~later[n])(functools.partial(start, tails[n]))
    for n in (0, 1, 2, 3, 4):
        pl.when(later[n])(functools.partial(start_late, n))

    region = (y % 4) * 3 + low
    lane = lax.broadcasted_iota(jnp.int32, (1, 128), 1)
    owners = jnp.full((1, 128), 0, jnp.int32)
    for e in range(32):
        owners = jnp.where(lane == e, owner[region, e], owners)
    rank = jnp.zeros((1, 128), jnp.int32)
    for e in range(32):
        rank += jnp.where((owners == owner[region, e]) & (lane > e), 1, 0)
    rank = jnp.minimum(rank, 3)
    slot = (((owners >> 1) - z) & 3) * 2 + ((owners + core) & 1)
    place_vmem[pl.ds(0, 1), :] = jnp.where(lane < 32, slot, 0)
    place_vmem[pl.ds(1, 1), :] = jnp.where(lane < 32, rank, 4) * 16
    placed = pltpu.make_async_copy(place_vmem, place, local_sem.at[2])
    placed.start()
    for n in range(8):
        right[pl.ds(n * GROUP + 8, 1)] = jnp.zeros((1, BLOCK, BLOCK), jnp.bfloat16)

    def ring(d, i, e, w, when):
        @at(when)
        def _():
            if i in alpha:
                e.wait_recv()
                need(d + 2, i, remote(left.at[d + 3, pl.ds(i, 1)], left.at[d + 2, pl.ds(i, 1)], east))
                need(d + 1, i, w)
            else:
                w.wait_recv()
                need(d + 2, i, remote(left.at[d + 1, pl.ds(i, 1)], left.at[d + 2, pl.ds(i, 1)], west))
                need(d + 3, i, e)

    codes = []
    if "x" in parts:
        for j in range(HALF):
            ring(0, alpha[j], to_e[alpha[j]], to_w[alpha[j]], 3 + 1.5 * j)
            ring(0, beta[j], to_e[beta[j]], to_w[beta[j]], 3 + 1.5 * j)

        @at(7.6)
        def _():
            code_e.wait_recv()
            codes.extend([remote(lcode.at[3], lcode.at[2], east), code_w])
    if "y" in parts:
        crossed = {}

        def crossing(j):
            @at(5 + 2.7 * j)
            def _():
                to_n[j].wait_recv()
                crossed[alpha[j]] = remote(row(relay, alpha[j]), left.at[4, pl.ds(alpha[j], 1)], north)
                to_s[j].wait_recv()
                crossed[beta[j]] = remote(row(relay, beta[j]), left.at[4, pl.ds(beta[j], 1)], south)
                if j == 0:
                    code_n.wait_recv()
                    crossed["code"] = remote(lcode.at[8], lcode.at[4], north)

            @at(14.5 + 2.7 * j)
            def _():
                for i in (alpha[j], beta[j]):
                    crossed[i].wait_recv()
                    if "x" not in parts:
                        continue
                    e = remote(left.at[4, pl.ds(i, 1)], left.at[7, pl.ds(i, 1)], east)
                    w = remote(left.at[4, pl.ds(i, 1)], left.at[5, pl.ds(i, 1)], west)
                    passed[i] = (e, w)
                if j == 0:
                    crossed["code"].wait_recv()
                    if "x" in parts:
                        passed["code"] = (
                            remote(lcode.at[4], lcode.at[7], east), remote(lcode.at[4], lcode.at[5], west))

            @at(20 + 3.5 * j)
            def _():
                if "x" not in parts:
                    return
                for i in (alpha[j], beta[j]):
                    e, w = passed[i]
                    if i in alpha:
                        e.wait_recv()
                        need(6, i, remote(left.at[7, pl.ds(i, 1)], left.at[6, pl.ds(i, 1)], east))
                        need(5, i, w)
                    else:
                        w.wait_recv()
                        need(6, i, remote(left.at[5, pl.ds(i, 1)], left.at[6, pl.ds(i, 1)], west))
                        need(7, i, e)
                if j == 0:
                    e, w = passed["code"]
                    e.wait_recv()
                    codes.extend([remote(lcode.at[7], lcode.at[6], east), w])

        passed = {}
        for j in range(HALF):
            crossing(j)

    if "z" in parts:
        at(4)(lambda: pl.when(later[5])(lambda: start_late(5)))
        at(9)(lambda: pl.when(later[6])(lambda: start_late(6)))
        over_up = [remote(rslot(3, 0, k), rslot(2, 0, k), up, False) for k in (0, 1)]
        over_down = [remote(rslot(1, 0, k), rslot(2, 0, k), down, False) for k in (2, 3)]
        over_code = remote(rcode.at[6], rcode.at[4], up, False)
        share_3 = [remote(rslot(3, 0, k), rslot(3, 1, k), twin, False) for k in (0, 1, 2, 3)]
        share_1 = [remote(rslot(1, 0, k), rslot(1, 1, k), twin, False) for k in (2, 3, 0, 1)]
        share_2 = [remote(rslot(2, 0, k), rslot(2, 1, k), twin, False) for k in (0, 1, 2, 3)]
        share_code = [remote(rcode.at[2 * d], rcode.at[2 * d + 1], twin, False) for d in (1, 2, 3)]

        def from_below(n):
            if n == 0:
                code_up.wait_recv()
                over_code.start()
                share_code[2].start()
            to_up[n].wait_recv()
            if n < 2:
                over_up[n].start()
            share_3[n].start()

        def from_above(n):
            if n == 0:
                code_down.wait_recv()
                share_code[0].start()
            to_down[n].wait_recv()
            if n < 2:
                over_down[n].start()
            share_1[n].start()

        def code_over():
            over_code.wait_recv()
            share_code[1].start()

        def from_across():
            for n, copy in enumerate(over_up + over_down):
                copy.wait_recv()
                share_2[n].start()

        for n in range(4):
            at((10, 16, 24, 27.2)[n])(functools.partial(lambda n: pl.when(z != 0)(lambda: from_below(n)), n))
            at((20, 25, 31.5, 31.6)[n])(functools.partial(lambda n: pl.when(z == 0)(lambda: from_below(n)), n))
            at((10.5, 16.5, 24, 27.2)[n])(functools.partial(from_above, n))
        at(20.5)(code_over)
        at(31.8)(from_across)

        def codes_done():
            code_twin.wait_recv()
            for copy in share_code + codes:
                copy.wait_recv()
            placed.wait()

        def right_done():
            own_right.wait()
            to_twin.wait_recv()
            for copy in share_3 + share_1 + share_2:
                copy.wait_recv()
    else:
        def right_done():
            pl.when(z != 3)(lambda: pl.semaphore_wait(ready.at[0], 1))
            pl.when(z == 0)(lambda: pl.semaphore_wait(ready.at[1], 1))
            own_right.wait()

        def codes_done():
            for copy in codes:
                copy.wait_recv()
            placed.wait()

    def picks(first):
        if first == 0:
            codes_done()

        @pl.loop(first, first + HALF)
        def _(i):
            for d in range(8):
                for s in range(SLOTS):
                    k = lcode[d, i * 2 + s]
                    where, at = place[0, k], place[1, k]
                    for t in range(OUT):
                        pick[i * 64 + (d * 2 + s) * 4 + t] = where * GROUP + rcode[where, at + ocode[i * 4 + t]]

    events.append((23.7, 900, lambda: picks(0)))
    events.append((27.1, 901, lambda: picks(HALF)))

    def product(i, ds, half):
        total = jnp.zeros((BLOCK, 2 * BLOCK), jnp.float32)
        for d in ds:
            lhs = jnp.concatenate([left[d, i, s] for s in range(SLOTS)], axis=1)
            rhs = jnp.concatenate([
                jnp.concatenate([right[pick[i * 64 + (d * 2 + s) * 4 + half * 2 + t]] for t in range(2)], axis=1)
                for s in range(SLOTS)], axis=0)
            total += jnp.dot(lhs, rhs, preferred_element_type=jnp.float32)
        return total

    def settle(ds, rows):
        for d in ds:
            for i in rows:
                for copy in pending.pop((d, i), []):
                    copy.wait_recv()

    for _, _, run in sorted(events, key=lambda e: e[:2]):
        run()
    own_left.wait()
    right_done()
    settle(range(4), range(ROWS))
    if "compute" in parts:
        @pl.loop(0, ROWS)
        def _(i):
            for half in range(2):
                acc[i, half] = product(i, range(4), half)
    for j in range(HALF):
        settle(range(4, 8), (j, j + HALF))
        if "compute" in parts:
            @pl.loop(0, 2)
            def _(h):
                i = j + h * HALF
                for half in range(2):
                    total = (acc[i, half] + product(i, range(4, 8), half)).astype(jnp.bfloat16)
                    for t in range(2):
                        stage[i, half * 2 + t] = total[:, t * BLOCK:(t + 1) * BLOCK]
                pltpu.make_async_copy(stage.at[i], out_hbm.at[i], out_sem.at[i]).start()
    if "compute" in parts:
        for i in range(ROWS):
            pltpu.make_async_copy(stage.at[i], out_hbm.at[i], out_sem.at[i]).wait()
    for copy in sent:
        copy.wait_send()


def solution(mesh, parts=PARTS):
    def step(*args):
        hbm = pl.BlockSpec(memory_space=pl.ANY)
        return pl.pallas_call(
            functools.partial(kernel, parts),
            out_shape=jax.ShapeDtypeStruct((ROWS, OUT, BLOCK, BLOCK), jnp.bfloat16),
            in_specs=[hbm] * 9,
            out_specs=hbm,
            scratch_shapes=[
                pltpu.VMEM((8, ROWS, SLOTS, BLOCK, BLOCK), jnp.bfloat16),
                pltpu.VMEM((ROWS, SLOTS, BLOCK, BLOCK), jnp.bfloat16),
                pltpu.VMEM((8 * GROUP, BLOCK, BLOCK), jnp.bfloat16),
                pltpu.VMEM((ROWS, 2, BLOCK, 2 * BLOCK), jnp.float32),
                pltpu.VMEM((ROWS, OUT, BLOCK, BLOCK), jnp.bfloat16),
                pltpu.SMEM((SLOTS, ROWS), jnp.int32),
                pltpu.SMEM((1, ROWS), jnp.int32),
                pltpu.SMEM((2, PANEL), jnp.int32),
                pltpu.SMEM((1, PANEL), jnp.int32),
                pltpu.SMEM((OUT, ROWS), jnp.int32),
                pltpu.SMEM((1, ROWS), jnp.int32),
                pltpu.SMEM((12, 32), jnp.int32),
                pltpu.SMEM((9, 128), jnp.int32),
                pltpu.SMEM((8, 128), jnp.int32),
                pltpu.SMEM((32,), jnp.int32),
                pltpu.VMEM((2, 128), jnp.int32),
                pltpu.SMEM((2, 128), jnp.int32),
                pltpu.SMEM((512,), jnp.int32),
                pltpu.SemaphoreType.DMA((N_COPIES,)),
                pltpu.SemaphoreType.DMA((N_COPIES,)),
                pltpu.SemaphoreType.DMA((3,)),
                pltpu.SemaphoreType.DMA((7,)),
                pltpu.SemaphoreType.DMA((ROWS,)),
                pltpu.SemaphoreType.REGULAR((7,)),
            ],
            compiler_params=pltpu.CompilerParams(
                collective_id=0, has_side_effects=True, vmem_limit_bytes=58 * 1024 * 1024
            ),
        )(args[0], args[1].T, args[2].T, args[3].reshape(8, BLOCK, BLOCK), args[4].T, args[5].T, args[6].T,
          args[7].T, args[8])

    whole = P("row", "col", None, None)
    flat = P("row", "col")
    return jax.shard_map(
        step, mesh=mesh, in_specs=(whole, flat, flat, whole, flat, flat, flat, flat, P()),
        out_specs=whole, check_vma=False,
    )
```

```python
import functools

import jax
import jax.numpy as jnp
from jax import lax
from jax.experimental import pallas as pl
from jax.experimental.pallas import tpu as pltpu
from jax.sharding import PartitionSpec as P

MESH = pl.DeviceIdType.MESH
ROWS, SLOTS, OUT, PANEL, BLOCK = 8, 2, 4, 4, 128
HALF = ROWS // 2
GROUP = 9
N_COPIES = 136
PARTS = ("x", "y", "z", "compute")


def kernel(
    parts,
    left_hbm, lcol_hbm, lcount_hbm, right_hbm, rcol_hbm, rcount_hbm, ocol_hbm, ocount_hbm, owner_hbm,
    out_hbm,
    left, relay, right, acc, stage,
    lcol, lcount, rcol, rcount, ocol, ocount, owner,
    lcode, rcode, ocode, place_vmem, place, pick,
    send_sem, recv_sem, local_sem, small_sem, out_sem, ready,
):
    r = lax.axis_index("row")
    c = lax.axis_index("col")
    z, core = r // 2, r % 2
    x, y, low = c // 24, (c // 3) % 8, c % 3

    def at_q(dx, dy):
        return (r, ((x + dx) % 4) * 24 + ((y + dy) % 8) * 3 + low)

    def at_row(dz, dcore):
        return (((z + dz) % 4) * 2 + (core + dcore) % 2, c)

    east, west, north, south = at_q(1, 0), at_q(3, 0), at_q(0, 2), at_q(0, 6)
    up, down, twin = at_row(1, 0), at_row(3, 0), at_row(0, 1)

    def is_first(dx, dy, dz, dc):
        return (
            ((x + dx) % 4 == 0) & ((y + dy) % 8 == 0) & (low == 0) & ((z + dz) % 4 == 0) & ((core + dc) % 2 == 0))

    first = is_first(0, 0, 0, 0)
    turn = y // 2
    neighbours = [east, west, north, south, twin, up, down]
    opposite = [1, 0, 3, 2, 4, 6, 5]
    later = [
        ((x != 3) | is_first(1, 0, 0, 0)) & ~first,
        ((x == 0) | is_first(3, 0, 0, 0)) & ~first,
        ((turn <= 1) | is_first(0, 2, 0, 0)) & ~first,
        ((turn == 0) | (turn == 3) | is_first(0, 6, 0, 0)) & ~first,
        ((core == 1) | is_first(0, 0, 0, 1)) & ~first,
        (z != 3) & ~first,
        (z == 0) | is_first(0, 0, 3, 0),
    ]
    barrier = pltpu.get_barrier_semaphore()

    def greet(device):
        pl.semaphore_signal(barrier, inc=1, device_id=device, device_id_type=MESH)

    def answer(n):
        pl.semaphore_signal(ready.at[opposite[n]], inc=1, device_id=neighbours[n], device_id_type=MESH)

    for n, device in enumerate(neighbours):
        pl.when(later[n])(functools.partial(greet, device))
    own_left = pltpu.make_async_copy(left_hbm, left.at[0], local_sem.at[0])
    own_left.start()
    own_right = pltpu.make_async_copy(right_hbm, right.at[pl.ds(0, 8)], local_sem.at[1])
    own_right.start()
    small = [
        pltpu.make_async_copy(src, dst, small_sem.at[n])
        for n, (src, dst) in enumerate((
            (lcol_hbm, lcol), (lcount_hbm, lcount), (rcol_hbm, rcol), (rcount_hbm, rcount),
            (ocol_hbm, ocol), (ocount_hbm, ocount), (owner_hbm, owner)))
    ]
    for copy in small:
        copy.start()
    earlier = sum(jnp.where(l, 0, 1) for l in later)
    pl.when(earlier > 0)(lambda: pl.semaphore_wait(barrier, earlier))
    for n in range(7):
        pl.when(~later[n])(functools.partial(answer, n))

    sent = []

    def remote(src, dst, device, start=True):
        n = len(sent)
        copy = pltpu.make_async_remote_copy(
            src_ref=src, dst_ref=dst, send_sem=send_sem.at[n], recv_sem=recv_sem.at[n],
            device_id=device, device_id_type=MESH,
        )
        if start:
            copy.start()
        sent.append(copy)
        return copy

    def row(ref, i):
        return ref.at[pl.ds(i, 1)]

    def rslot(dz, dc, k):
        return right.at[pl.ds((dz * 2 + dc) * GROUP + k * 2, 2)]

    events = []
    pending = {}

    def need(d, i, copy):
        pending.setdefault((d, i), []).append(copy)

    def at(when):
        return lambda run: events.append((when, len(events), run))

    order_e = list(range(ROWS))
    order_w = list(range(HALF, ROWS)) + list(range(HALF))
    alpha, beta = order_e[:HALF], order_e[HALF:]
    code_up = remote(rcode.at[0], rcode.at[6], up, False)
    code_down = remote(rcode.at[0], rcode.at[2], down, False)
    code_twin = remote(rcode.at[0], rcode.at[1], twin, False)
    code_e = remote(lcode.at[0], lcode.at[3], east, False)
    code_w = remote(lcode.at[0], lcode.at[1], west, False)
    code_n = remote(lcode.at[0], lcode.at[8], north, False)
    to_up = [remote(right_hbm.at[pl.ds(2 * k, 2)], rslot(3, 0, k), up, False) for k in (0, 1, 2, 3)]
    to_down = [remote(right_hbm.at[pl.ds(2 * k, 2)], rslot(1, 0, k), down, False) for k in (2, 3, 0, 1)]
    to_e = {i: remote(row(left_hbm, i), left.at[3, pl.ds(i, 1)], east, False) for i in order_e}
    to_w = {i: remote(row(left_hbm, i), left.at[1, pl.ds(i, 1)], west, False) for i in order_w}
    to_n = [remote(row(left_hbm, i), row(relay, i), north, False) for i in alpha]
    to_s = [remote(row(left_hbm, i), row(relay, i), south, False) for i in beta]
    to_twin = remote(right_hbm, right.at[pl.ds(GROUP, 8)], twin, False)
    east_rows, west_rows = list(to_e.values()), list(to_w.values())
    heads = [east_rows[:1], west_rows[:1], [], [], [], to_up[:0], to_down[:0]]
    tails = [
        [code_e] + east_rows[1:], [code_w] + west_rows[1:], [code_n] + to_n, to_s,
        [code_twin, to_twin], [code_up] + to_up[0:], [code_down] + to_down[0:]]

    def start(copies):
        for copy in copies:
            copy.start()

    def start_late(n):
        pl.semaphore_wait(ready.at[n], 1)
        start(heads[n] + tails[n])

    for n in (5, 6, 0, 1):
        pl.when(~later[n])(functools.partial(start, heads[n]))
    for copy in small:
        copy.wait()
    panel = (r + x * 2 + y // 4) % 8
    for i in range(ROWS):
        for s in range(SLOTS):
            lcode[0, i * 2 + s] = jnp.where(s < lcount[0, i], panel * 4 + lcol[s, i], 32)
        for t in range(OUT):
            ocode[i * 4 + t] = jnp.where(t < ocount[0, i], ocol[t, i], 8)
    for k in range(PANEL):
        c0 = jnp.where(0 < rcount[0, k], rcol[0, k], -1)
        c1 = jnp.where(1 < rcount[0, k], rcol[1, k], -1)
        for n in range(8):
            rcode[0, k * 16 + n] = jnp.where(c0 == n, k * 2, jnp.where(c1 == n, k * 2 + 1, 8))
        rcode[0, k * 16 + 8] = 8
    for n in range(9):
        rcode[0, PANEL * 16 + n] = 8
    for n in (5, 6, 0, 1, 2, 3, 4):
        pl.when(~later[n])(functools.partial(start, tails[n]))
    for n in (0, 1, 2, 3, 4):
        pl.when(later[n])(functools.partial(start_late, n))

    region = (y % 4) * 3 + low
    lane = lax.broadcasted_iota(jnp.int32, (1, 128), 1)
    owners = jnp.full((1, 128), 0, jnp.int32)
    for e in range(32):
        owners = jnp.where(lane == e, owner[region, e], owners)
    rank = jnp.zeros((1, 128), jnp.int32)
    for e in range(32):
        rank += jnp.where((owners == owner[region, e]) & (lane > e), 1, 0)
    rank = jnp.minimum(rank, 3)
    slot = (((owners >> 1) - z) & 3) * 2 + ((owners + core) & 1)
    place_vmem[pl.ds(0, 1), :] = jnp.where(lane < 32, slot, 0)
    place_vmem[pl.ds(1, 1), :] = jnp.where(lane < 32, rank, 4) * 16
    placed = pltpu.make_async_copy(place_vmem, place, local_sem.at[2])
    placed.start()
    for n in range(8):
        right[pl.ds(n * GROUP + 8, 1)] = jnp.zeros((1, BLOCK, BLOCK), jnp.bfloat16)

    def ring(d, i, e, w, when):
        @at(when)
        def _():
            if i in alpha:
                e.wait_recv()
                need(d + 2, i, remote(left.at[d + 3, pl.ds(i, 1)], left.at[d + 2, pl.ds(i, 1)], east))
                need(d + 1, i, w)
            else:
                w.wait_recv()
                need(d + 2, i, remote(left.at[d + 1, pl.ds(i, 1)], left.at[d + 2, pl.ds(i, 1)], west))
                need(d + 3, i, e)

    codes = []
    if "x" in parts:
        for j in range(HALF):
            ring(0, alpha[j], to_e[alpha[j]], to_w[alpha[j]], 3 + 1.5 * j)
            ring(0, beta[j], to_e[beta[j]], to_w[beta[j]], 3 + 1.5 * j)

        @at(7.6)
        def _():
            code_e.wait_recv()
            codes.extend([remote(lcode.at[3], lcode.at[2], east), code_w])
    if "y" in parts:
        crossed = {}

        def crossing(j):
            @at(5 + 2.7 * j)
            def _():
                to_n[j].wait_recv()
                crossed[alpha[j]] = remote(row(relay, alpha[j]), left.at[4, pl.ds(alpha[j], 1)], north)
                to_s[j].wait_recv()
                crossed[beta[j]] = remote(row(relay, beta[j]), left.at[4, pl.ds(beta[j], 1)], south)
                if j == 0:
                    code_n.wait_recv()
                    crossed["code"] = remote(lcode.at[8], lcode.at[4], north)

            @at(14.5 + 2.7 * j)
            def _():
                for i in (alpha[j], beta[j]):
                    crossed[i].wait_recv()
                    if "x" not in parts:
                        continue
                    e = remote(left.at[4, pl.ds(i, 1)], left.at[7, pl.ds(i, 1)], east)
                    w = remote(left.at[4, pl.ds(i, 1)], left.at[5, pl.ds(i, 1)], west)
                    passed[i] = (e, w)
                if j == 0:
                    crossed["code"].wait_recv()
                    if "x" in parts:
                        passed["code"] = (
                            remote(lcode.at[4], lcode.at[7], east), remote(lcode.at[4], lcode.at[5], west))

            @at(20 + 3.5 * j)
            def _():
                if "x" not in parts:
                    return
                for i in (alpha[j], beta[j]):
                    e, w = passed[i]
                    if i in alpha:
                        e.wait_recv()
                        need(6, i, remote(left.at[7, pl.ds(i, 1)], left.at[6, pl.ds(i, 1)], east))
                        need(5, i, w)
                    else:
                        w.wait_recv()
                        need(6, i, remote(left.at[5, pl.ds(i, 1)], left.at[6, pl.ds(i, 1)], west))
                        need(7, i, e)
                if j == 0:
                    e, w = passed["code"]
                    e.wait_recv()
                    codes.extend([remote(lcode.at[7], lcode.at[6], east), w])

        passed = {}
        for j in range(HALF):
            crossing(j)

    if "z" in parts:
        at(4)(lambda: pl.when(later[5])(lambda: start_late(5)))
        at(9)(lambda: pl.when(later[6])(lambda: start_late(6)))
        over_up = [remote(rslot(3, 0, k), rslot(2, 0, k), up, False) for k in (0, 1)]
        over_down = [remote(rslot(1, 0, k), rslot(2, 0, k), down, False) for k in (2, 3)]
        over_code = remote(rcode.at[6], rcode.at[4], up, False)
        share_3 = [remote(rslot(3, 0, k), rslot(3, 1, k), twin, False) for k in (0, 1, 2, 3)]
        share_1 = [remote(rslot(1, 0, k), rslot(1, 1, k), twin, False) for k in (2, 3, 0, 1)]
        share_2 = [remote(rslot(2, 0, k), rslot(2, 1, k), twin, False) for k in (0, 1, 2, 3)]
        share_code = [remote(rcode.at[2 * d], rcode.at[2 * d + 1], twin, False) for d in (1, 2, 3)]

        def from_below(n):
            if n == 0:
                code_up.wait_recv()
                over_code.start()
                share_code[2].start()
            to_up[n].wait_recv()
            if n < 2:
                over_up[n].start()
            share_3[n].start()

        def from_above(n):
            if n == 0:
                code_down.wait_recv()
                share_code[0].start()
            to_down[n].wait_recv()
            if n < 2:
                over_down[n].start()
            share_1[n].start()

        def code_over():
            over_code.wait_recv()
            share_code[1].start()

        def from_across():
            for n, copy in enumerate(over_up + over_down):
                copy.wait_recv()
                share_2[n].start()

        for n in range(4):
            at((10, 16, 24, 27.2)[n])(functools.partial(lambda n: pl.when(z != 0)(lambda: from_below(n)), n))
            at((20, 25, 31.5, 31.6)[n])(functools.partial(lambda n: pl.when(z == 0)(lambda: from_below(n)), n))
            at((10.5, 16.5, 24, 27.2)[n])(functools.partial(from_above, n))
        at(20.5)(code_over)
        at(27.25)(lambda: pl.when(z >= 2)(from_across))
        at(30.2)(lambda: pl.when(z == 1)(from_across))
        at(31.8)(lambda: pl.when(z == 0)(from_across))

        def codes_done():
            code_twin.wait_recv()
            for copy in share_code + codes:
                copy.wait_recv()
            placed.wait()

        def right_done():
            own_right.wait()
            to_twin.wait_recv()
            for copy in share_3 + share_1 + share_2:
                copy.wait_recv()
    else:
        def right_done():
            pl.when(z != 3)(lambda: pl.semaphore_wait(ready.at[0], 1))
            pl.when(z == 0)(lambda: pl.semaphore_wait(ready.at[1], 1))
            own_right.wait()

        def codes_done():
            for copy in codes:
                copy.wait_recv()
            placed.wait()

    def picks(first):
        if first == 0:
            codes_done()

        @pl.loop(first, first + HALF)
        def _(i):
            for d in range(8):
                for s in range(SLOTS):
                    k = lcode[d, i * 2 + s]
                    where, at = place[0, k], place[1, k]
                    for t in range(OUT):
                        pick[i * 64 + (d * 2 + s) * 4 + t] = where * GROUP + rcode[where, at + ocode[i * 4 + t]]

    events.append((23.7, 900, lambda: picks(0)))
    events.append((27.1, 901, lambda: picks(HALF)))

    def product(i, ds, half):
        total = jnp.zeros((BLOCK, 2 * BLOCK), jnp.float32)
        for d in ds:
            lhs = jnp.concatenate([left[d, i, s] for s in range(SLOTS)], axis=1)
            rhs = jnp.concatenate([
                jnp.concatenate([right[pick[i * 64 + (d * 2 + s) * 4 + half * 2 + t]] for t in range(2)], axis=1)
                for s in range(SLOTS)], axis=0)
            total += jnp.dot(lhs, rhs, preferred_element_type=jnp.float32)
        return total

    gone = []

    @at(30.3)
    def _():
        for copies in (heads[0], tails[0], heads[1], tails[1], tails[2], tails[3], tails[4]):
            gone.extend(copies)
        for copy in gone:
            copy.wait_send()

    def settle(ds, rows):
        for d in ds:
            for i in rows:
                for copy in pending.pop((d, i), []):
                    copy.wait_recv()

    for _, _, run in sorted(events, key=lambda e: e[:2]):
        run()
    own_left.wait()
    right_done()
    settle(range(4), range(ROWS))
    if "compute" in parts:
        @pl.loop(0, ROWS)
        def _(i):
            for half in range(2):
                acc[i, half] = product(i, range(4), half)
    for j in range(HALF):
        settle(range(4, 8), (j, j + HALF))
        if "compute" in parts:
            @pl.loop(0, 2)
            def _(h):
                i = j + h * HALF
                for half in range(2):
                    total = (acc[i, half] + product(i, range(4, 8), half)).astype(jnp.bfloat16)
                    for t in range(2):
                        stage[i, half * 2 + t] = total[:, t * BLOCK:(t + 1) * BLOCK]
                pltpu.make_async_copy(stage.at[i], out_hbm.at[i], out_sem.at[i]).start()
    for copy in sent:
        if not any(copy is other for other in gone):
            copy.wait_send()
    if "compute" in parts:
        for i in range(ROWS):
            pltpu.make_async_copy(stage.at[i], out_hbm.at[i], out_sem.at[i]).wait()


def solution(mesh, parts=PARTS):
    def step(*args):
        hbm = pl.BlockSpec(memory_space=pl.ANY)
        return pl.pallas_call(
            functools.partial(kernel, parts),
            out_shape=jax.ShapeDtypeStruct((ROWS, OUT, BLOCK, BLOCK), jnp.bfloat16),
            in_specs=[hbm] * 9,
            out_specs=hbm,
            scratch_shapes=[
                pltpu.VMEM((8, ROWS, SLOTS, BLOCK, BLOCK), jnp.bfloat16),
                pltpu.VMEM((ROWS, SLOTS, BLOCK, BLOCK), jnp.bfloat16),
                pltpu.VMEM((8 * GROUP, BLOCK, BLOCK), jnp.bfloat16),
                pltpu.VMEM((ROWS, 2, BLOCK, 2 * BLOCK), jnp.float32),
                pltpu.VMEM((ROWS, OUT, BLOCK, BLOCK), jnp.bfloat16),
                pltpu.SMEM((SLOTS, ROWS), jnp.int32),
                pltpu.SMEM((1, ROWS), jnp.int32),
                pltpu.SMEM((2, PANEL), jnp.int32),
                pltpu.SMEM((1, PANEL), jnp.int32),
                pltpu.SMEM((OUT, ROWS), jnp.int32),
                pltpu.SMEM((1, ROWS), jnp.int32),
                pltpu.SMEM((12, 32), jnp.int32),
                pltpu.SMEM((9, 128), jnp.int32),
                pltpu.SMEM((8, 128), jnp.int32),
                pltpu.SMEM((32,), jnp.int32),
                pltpu.VMEM((2, 128), jnp.int32),
                pltpu.SMEM((2, 128), jnp.int32),
                pltpu.SMEM((512,), jnp.int32),
                pltpu.SemaphoreType.DMA((N_COPIES,)),
                pltpu.SemaphoreType.DMA((N_COPIES,)),
                pltpu.SemaphoreType.DMA((3,)),
                pltpu.SemaphoreType.DMA((7,)),
                pltpu.SemaphoreType.DMA((ROWS,)),
                pltpu.SemaphoreType.REGULAR((7,)),
            ],
            compiler_params=pltpu.CompilerParams(
                collective_id=0, has_side_effects=True, vmem_limit_bytes=58 * 1024 * 1024
            ),
        )(args[0], args[1].T, args[2].T, args[3].reshape(8, BLOCK, BLOCK), args[4].T, args[5].T, args[6].T,
          args[7].T, args[8])

    whole = P("row", "col", None, None)
    flat = P("row", "col")
    return jax.shard_map(
        step, mesh=mesh, in_specs=(whole, flat, flat, whole, flat, flat, flat, flat, P()),
        out_specs=whole, check_vma=False,
    )
```
